32 devices in a mesh: energy: 2 (over x), mom: 16 (over z, y, core).
Axes of the slice: x: 2, y: 2, z: 4, core: 2. Of those that a mesh axis runs over, the one named last changes fastest.
Arguments:
- source: float32 [256, 128, 1024], P(('energy', 'mom')), parts along dimension 0, may hold values from -6 to 6
- green: float32 [256, 1024], P(('energy', 'mom')), parts along dimension 0, may hold values from 0.1 to 0.6
- couple_one: float32 [2, 4, 128, 128], replicated, may hold values from -0.5 to 0.5
- couple_two: float32 [2, 4, 128, 128], replicated, may hold values from -0.5 to 0.5
- p_bracket: int32 [2, 1024], replicated, may hold values from 0 to 28
- q_bracket: int32 [2, 1024], replicated, may hold values from 0 to 28
- p_weight: float32 [2, 4, 1024], replicated, may hold values from -0.25 to 1
- q_weight: float32 [2, 4, 1024], replicated, may hold values from -0.25 to 1
- qr_bracket: int32 [2, 1024], replicated, may hold values from 0 to 28
- r_bracket: int32 [2, 1024], replicated, may hold values from 0 to 28
- qr_weight: float32 [2, 4, 1024], replicated, may hold values from -0.25 to 1
- r_weight: float32 [2, 4, 1024], replicated, may hold values from -0.25 to 1
Outputs:
- amplitude: float32 [256, 128, 1024], P(('energy', 'mom')), parts along dimension 0
- component: float32 [256, 128, 1024], P(('energy', 'mom')), parts along dimension 0
The draws below stay inside these ranges and needn't reach their ends.
There are 2 independent parts, one for each index of `energy`. The reference program is written for one: setup_inputs(seed, part) draws one part's arguments, and reference() takes and returns one part's arrays. A program takes and returns all parts, laid end to end along the dimension named above; an argument that names none is the same for every part. Nothing has to cross between parts.
All inputs are finite; a program needn't handle non-finite values.
Results may differ from the reference program's by a relative error of at most 0.0001.
Values sent between devices are 32-bit elements; how exact they have to be, the bound alone decides.
A program may use at most 128 MiB of HBM per device.

```python
import math
import jax
import jax.numpy as jnp
from jax import lax

P_SIZE = 32
Q = 32
R = 32
CH = 128
K = 2
ITERS = 2


def touch_ends(values, rng, low, top_value):
    longest = values.shape.index(max(values.shape))
    spots = []
    for shift in (0, 1):
        where = [jax.random.randint(jax.random.fold_in(rng, axis), (), 0, length) for axis, length in enumerate(values.shape)]
        where[longest] = (where[longest] + shift) % values.shape[longest]
        spots.append(tuple(where))
    return values.at[spots[0]].set(low).at[spots[1]].set(top_value)


def levels(rng, dims, pieces, smallest, top_value):
    loudness, own = 1.0, jax.random.fold_in(rng, 6)
    for position, blocks in pieces:
        draws = jnp.exp(jax.random.uniform(jax.random.fold_in(own, position), (blocks,), jnp.float32, smallest / len(pieces), top_value / len(pieces)))
        loudness = loudness * jnp.repeat(draws, dims[position] // blocks).reshape([-1 if axis == position else 1 for axis in range(len(dims))])
    return loudness


def noise(key, dims, width, limit, shards=(), held_as=jnp.bfloat16):
    loudness = levels(key, dims, shards, -0.22, 0.18) if shards else 1.0
    array = jax.random.normal(key, dims, jnp.float32) * width * loudness
    return jnp.minimum(jnp.maximum(array, -limit), limit).astype(held_as)


def setup_inputs(seed: int = 0, part: int = 0) -> dict:
    key_list = jax.random.split(jax.random.key(seed), 13)
    part_splits = jax.random.split(jax.random.fold_in(key_list[12], part), 13)
    return {
        "source": noise(part_splits[0], (4 * R, CH, P_SIZE * Q), 1.0, 6.0, ((0, 16),), jnp.float32),
        "green": jnp.clip(jnp.exp(math.log(0.6) - 1.7917595 * jax.random.uniform(part_splits[1], (4 * P_SIZE, Q * R), jnp.float32) ** levels(part_splits[1], (4 * P_SIZE, Q * R), ((0, 16),), -0.2, 0.2)), 0.1, 0.6),
        "couple_one": noise(key_list[2], (K, 4, CH, CH), CH ** -0.5, 0.5, (), jnp.float32),
        "couple_two": noise(key_list[3], (K, 4, CH, CH), CH ** -0.5, 0.5, (), jnp.float32),
        "p_bracket": touch_ends(jax.random.randint(key_list[4], (K, P_SIZE * Q), 0, P_SIZE - 3), jax.random.fold_in(key_list[4], 1), 0, (P_SIZE - 3) - 1).astype(jnp.int32),
        "q_bracket": touch_ends(jax.random.randint(key_list[5], (K, P_SIZE * Q), 0, Q - 3), jax.random.fold_in(key_list[5], 1), 0, (Q - 3) - 1).astype(jnp.int32),
        "p_weight": jnp.clip(jax.random.uniform(key_list[6], (K, 4, P_SIZE * Q), jnp.float32, -0.25, 1.0), -0.25, 1.0),
        "q_weight": jnp.clip(jax.random.uniform(key_list[7], (K, 4, P_SIZE * Q), jnp.float32, -0.25, 1.0), -0.25, 1.0),
        "qr_bracket": touch_ends(jax.random.randint(key_list[8], (K, Q * R), 0, Q - 3), jax.random.fold_in(key_list[8], 1), 0, (Q - 3) - 1).astype(jnp.int32),
        "r_bracket": touch_ends(jax.random.randint(key_list[9], (K, Q * R), 0, R - 3), jax.random.fold_in(key_list[9], 1), 0, (R - 3) - 1).astype(jnp.int32),
        "qr_weight": jnp.clip(jax.random.uniform(key_list[10], (K, 4, Q * R), jnp.float32, -0.25, 1.0), -0.25, 1.0),
        "r_weight": jnp.clip(jax.random.uniform(key_list[11], (K, 4, Q * R), jnp.float32, -0.25, 1.0), -0.25, 1.0),
    }


def spline_matrix(first_index, second_index, first_weight, second_weight, first_count, second_count):
    first_grid = jnp.arange(first_count, dtype=jnp.int32)[None, :] - first_index[:, None]
    second_grid = jnp.arange(second_count, dtype=jnp.int32)[None, :] - second_index[:, None]
    first_rows = jnp.zeros(first_grid.shape, jnp.float32)
    second_rows = jnp.zeros(second_grid.shape, jnp.float32)
    for offset in range(4):
        first_rows = first_rows + jnp.where(first_grid == offset, first_weight[offset][:, None], jnp.float32(0.0))
        second_rows = second_rows + jnp.where(second_grid == offset, second_weight[offset][:, None], jnp.float32(0.0))
    return (first_rows[:, :, None] * second_rows[:, None, :]).reshape(first_index.shape[0], first_count * second_count)


def class_mats(couple, row_count, start):
    classes = (start + jnp.arange(row_count, dtype=jnp.int32)) % 4
    select = jax.nn.one_hot(classes, 4, dtype=jnp.float32)
    return jnp.einsum('rc,cmn->rmn', select, couple, precision=lax.Precision.HIGHEST)


def mix(mats, values):
    return jnp.einsum('rmn,rnx->rmx', mats, values, precision=lax.Precision.HIGHEST)


def interp(values, smat):
    return jnp.einsum('rcx,yx->rcy', values, smat, precision=lax.Precision.HIGHEST)


def reference(source, green, couple_one, couple_two, p_bracket, q_bracket, p_weight, q_weight, qr_bracket, r_bracket, qr_weight, r_weight):
    quarter = CH // 4
    first_maps = [spline_matrix(p_bracket[k], q_bracket[k], p_weight[k], q_weight[k], P_SIZE, Q) for k in range(K)]
    second_maps = [spline_matrix(qr_bracket[k], r_bracket[k], qr_weight[k], r_weight[k], Q, R) for k in range(K)]
    mats_one = [class_mats(couple_one[k], 4 * R, 0) for k in range(K)]
    mats_two = [class_mats(couple_two[k], 4 * P_SIZE, 0) for k in range(K)]
    state = source
    component = None
    for step in range(ITERS):
        one = interp(mix(mats_one[0], state), first_maps[0])
        for k in range(1, K):
            one = one + interp(mix(mats_one[k], state), first_maps[k])
        regrouped = one.reshape(R, 4, 4, quarter, P_SIZE, Q).transpose(4, 2, 3, 1, 5, 0).reshape(4 * P_SIZE, CH, Q * R)
        total = mix(mats_two[0], interp(regrouped, second_maps[0]))
        for k in range(1, K):
            total = total + mix(mats_two[k], interp(regrouped, second_maps[k]))
        component = green[:, None, :] * total
        back = component.reshape(P_SIZE, 4, quarter, 4, Q, R).transpose(5, 3, 1, 2, 0, 4).reshape(4 * R, CH, P_SIZE * Q)
        state = source + back
    return state, component
```

```python
import functools

import jax
import jax.numpy as jnp
from jax import lax
from jax.experimental import pallas as pl
from jax.experimental.pallas import tpu as pltpu
from jax.sharding import PartitionSpec as P

K = 2
ITERS = 2
LANES = 128
F32 = jnp.float32
BF16 = jnp.bfloat16


def split(values):
    high = values.astype(BF16)
    return high, (values - high.astype(F32)).astype(BF16)


def dot3(a_high, a_low, b_high, b_low, dims=(((1,), (0,)), ((), ()))):
    mul = functools.partial(lax.dot_general, dimension_numbers=dims, preferred_element_type=F32)
    return mul(a_high, b_high) + (mul(a_high, b_low) + mul(a_low, b_high))


def sweep_kernel(
    n,
    quarter,
    q_size,
    tab_ref,
    green_t_ref,
    green_ref,
    mix_one_ref,
    mix_two_ref,
    mix_nat_ref,
    source_ref,
    amp_ref,
    comp_ref,
    map_high,
    map_low,
    start_t,
    send_buf,
    recv_one,
    recv_two,
    v_high,
    v_low,
    w_high,
    w_low,
    w_keep,
    e_high,
    e_low,
    d_high,
    d_low,
    a_high,
    a_low,
    load_sem,
    send_sem,
    recv_sem,
):
    me = lax.axis_index("mom")
    grid = start_t.shape[1]
    groups = start_t.shape[0]
    local = start_t.shape[2] // LANES
    block = 2 * LANES
    blocks = grid // block
    block_dests = n // blocks
    per_tile = LANES // q_size

    load = pltpu.make_async_copy(source_ref, amp_ref, load_sem)
    load.start()

    barrier = pltpu.get_barrier_semaphore()

    def greet(offset, carry):
        pl.semaphore_signal(
            barrier,
            inc=1,
            device_id={"mom": lax.rem(me + offset, n)},
            device_id_type=pl.DeviceIdType.MESH,
        )
        return carry

    lax.fori_loop(1, n, greet, 0)

    def rows_of(i, size=block):
        return pl.ds(pl.multiple_of(i * size, size), size)

    def build_map(slot):
        base = 10 * slot

        def body(i, carry):
            rows = rows_of(i)
            table = tab_ref[rows, :]

            def col(j):
                return jnp.broadcast_to(table[:, base + j : base + j + 1], (block, LANES))

            first, second = col(0), col(1)
            w_first = [col(2 + j) for j in range(4)]
            w_second = [col(6 + j) for j in range(4)]
            lane = lax.broadcasted_iota(jnp.int32, (block, LANES), 1)
            fine = (lane % q_size).astype(F32) - second
            coarse = (lane // q_size).astype(F32) - first
            zero = jnp.zeros((block, LANES), F32)
            inner = zero
            for j in range(4):
                inner = inner + jnp.where(fine == j, w_second[j], zero)
            for t in range(grid // LANES):
                here = coarse + F32(per_tile * t)
                outer = zero
                for j in range(4):
                    outer = outer + jnp.where(here == j, w_first[j], zero)
                high, low = split(outer * inner)
                map_high[slot, rows, t * LANES : (t + 1) * LANES] = high
                map_low[slot, rows, t * LANES : (t + 1) * LANES] = low
            return carry

        lax.fori_loop(0, blocks, body, 0)

    def copy_of(phase, g, offset):
        dest = lax.rem(me + offset, n)
        into = recv_one if phase == 0 else recv_two
        return pltpu.make_async_remote_copy(
            src_ref=send_buf.at[g, dest],
            dst_ref=into.at[g, me],
            send_sem=send_sem.at[g, offset],
            recv_sem=recv_sem.at[phase, g, offset],
            device_id={"mom": dest},
            device_id_type=pl.DeviceIdType.MESH,
        )

    def start_sends(phase, g):
        def body(offset, carry):
            copy_of(phase, g, offset).start()
            return carry

        lax.fori_loop(1, n, body, 0)
        into = recv_one if phase == 0 else recv_two
        into[g, me] = send_buf[g, me]

    def wait_sends(phase, g):
        def body(offset, carry):
            copy_of(phase, g, offset).wait_send()
            return carry

        lax.fori_loop(1, n, body, 0)

    def wait_recvs(phase, g):
        into = recv_one if phase == 0 else recv_two

        def body(offset, carry):
            origin = lax.rem(me + n - offset, n)
            pltpu.make_async_remote_copy(
                src_ref=send_buf.at[g, origin],
                dst_ref=into.at[g, origin],
                send_sem=send_sem.at[g, offset],
                recv_sem=recv_sem.at[phase, g, offset],
                device_id={"mom": origin},
                device_id_type=pl.DeviceIdType.MESH,
            ).wait_recv()
            return carry

        lax.fori_loop(1, n, body, 0)

    def set_values(values):
        high, low = split(values)
        v_high[...] = high
        v_low[...] = low

    def place(g, i, part, out):
        out = out.reshape(block_dests, local, q_size, LANES)
        dests = pl.ds(i * block_dests, block_dests)
        for other in range(local):
            send_buf[
                g,
                dests,
                part * q_size : (part + 1) * q_size,
                other * LANES : (other + 1) * LANES,
            ] = out[:, other]

    def one_in(it):
        def body(g, carry):
            if it == 0:
                set_values(start_t[g])
            else:
                wait_recvs(1, g)
                set_values(start_t[g] + recv_two[g].reshape(grid, local * LANES))

            def rows_body(i, inner):
                rows = rows_of(i)
                for k in range(K):
                    out = dot3(map_high[k, rows, :], map_low[k, rows, :], v_high[...], v_low[...])
                    high, low = split(out)
                    lanes = pl.ds(pl.multiple_of((k * groups + g) * LANES, LANES), LANES)
                    for part in range(local):
                        w_high[part, rows, lanes] = high[:, part * LANES : (part + 1) * LANES]
                        w_low[part, rows, lanes] = low[:, part * LANES : (part + 1) * LANES]
                return inner

            lax.fori_loop(0, blocks, rows_body, 0)
            return carry

        lax.fori_loop(0, groups, body, 0)

    def one_out(it):
        def body(g, carry):
            if it > 0:
                wait_sends(1, g)

            def rows_body(i, inner):
                rows = rows_of(i)
                for part in range(local):
                    out = dot3(w_high[part, rows, :], w_low[part, rows, :], e_high[g], e_low[g])
                    place(g, i, part, out)
                return inner

            lax.fori_loop(0, blocks, rows_body, 0)
            start_sends(0, g)
            return carry

        lax.fori_loop(0, groups, body, 0)

    def two(it):
        last = it == ITERS - 1

        def body(g, carry):
            wait_recvs(0, g)
            wait_sends(0, g)
            set_values(recv_one[g].reshape(grid, local * LANES))

            def rows_body(i, inner):
                rows = rows_of(i)
                outs = [
                    dot3(
                        map_high[K + k, rows, :], map_low[K + k, rows, :], v_high[...], v_low[...]
                    )
                    for k in range(K)
                ]
                for part in range(local):
                    lanes = slice(part * LANES, (part + 1) * LANES)
                    joined = jnp.concatenate([out[:, lanes] for out in outs], axis=1)
                    high, low = split(joined)
                    mixed = dot3(high, low, d_high[g], d_low[g])
                    place(g, i, part, mixed * green_t_ref[g, rows, part : part + 1])
                    if last:
                        for k in range(K):
                            w_keep[part, k, rows, :] = outs[k][:, lanes]
                return inner

            lax.fori_loop(0, blocks, rows_body, 0)
            start_sends(1, g)
            if last:
                outer = grid // q_size
                for part in range(local):
                    scale = green_ref[pl.ds(part * groups + g, 1), :]
                    for s in range(blocks):
                        step = block // outer
                        joined = jnp.concatenate(
                            [
                                jnp.concatenate(
                                    [
                                        w_keep[part, k, pl.ds(q, outer, stride=q_size), :]
                                        for q in range(s * step, (s + 1) * step)
                                    ],
                                    axis=0,
                                )
                                for k in range(K)
                            ],
                            axis=1,
                        )
                        high, low = split(joined)
                        out = dot3(a_high[g], a_low[g], high, low, (((1,), (1,)), ((), ())))
                        lanes = slice(s * block, (s + 1) * block)
                        comp_ref[part * groups + g, :, lanes] = out * scale[:, lanes]
            return carry

        lax.fori_loop(0, groups, body, 0)

    for k in range(K):
        build_map(k)
    for g in range(groups):
        e_high[g], e_low[g] = split(mix_one_ref[g])
        d_high[g], d_low[g] = split(mix_two_ref[g])
        a_high[g], a_low[g] = split(mix_nat_ref[g])
    load.wait()

    def transpose_in(g, carry):
        chans = pl.ds(pl.multiple_of(g * quarter, quarter), quarter)
        for part in range(local):
            stacked = jnp.concatenate(
                [amp_ref[part * groups + c, chans, :] for c in range(groups)], axis=0
            )
            start_t[g, :, part * LANES : (part + 1) * LANES] = stacked.T
        return carry

    lax.fori_loop(0, groups, transpose_in, 0)

    for it in range(ITERS):
        one_in(it)
        if it == 0:
            pl.semaphore_wait(barrier, n - 1)
        one_out(it)
        if it == 0:
            for k in range(K):
                build_map(K + k)
        two(it)

    def finish(g, carry):
        wait_recvs(1, g)
        total = start_t[g] + recv_two[g].reshape(grid, local * LANES)
        chans = pl.ds(pl.multiple_of(g * quarter, quarter), quarter)
        for part in range(local):
            turned = total[:, part * LANES : (part + 1) * LANES].T
            for c in range(groups):
                amp_ref[part * groups + c, chans, :] = turned[c * quarter : (c + 1) * quarter]
        wait_sends(1, g)
        return carry

    lax.fori_loop(0, groups, finish, 0)


def fused(
    n,
    source,
    green,
    couple_one,
    couple_two,
    p_bracket,
    q_bracket,
    p_weight,
    q_weight,
    qr_bracket,
    r_bracket,
    qr_weight,
    r_weight,
):
    rows, channels, grid = source.shape
    groups = couple_one.shape[1]
    quarter = channels // groups
    local = rows // groups
    r_size = rows * n // groups
    q_size = grid // r_size

    def turn(values):
        lead = values.shape[:-1]
        return jnp.swapaxes(values.reshape(lead + (q_size, r_size)), -1, -2).reshape(values.shape)

    columns = []
    for k in range(K):
        columns += [p_bracket[k][None].astype(F32), q_bracket[k][None].astype(F32), p_weight[k], q_weight[k]]
    for k in range(K):
        columns += [
            turn(r_bracket[k])[None].astype(F32),
            turn(qr_bracket[k])[None].astype(F32),
            turn(r_weight[k]),
            turn(qr_weight[k]),
        ]
    table = jnp.concatenate(columns, axis=0)
    table = jnp.pad(table, ((0, LANES - table.shape[0]), (0, 0))).T
    green_t = turn(green).reshape(local, groups, grid).transpose(1, 2, 0)

    eye = jnp.eye(groups, dtype=bool)[None, None, None, :, None, :, None]
    blocks = couple_one.reshape(K, groups, groups, quarter, groups, quarter).transpose(2, 0, 4, 1, 5, 3)
    mix_one = jnp.where(eye, blocks[:, :, :, :, :, None, :], F32(0.0)).reshape(
        groups, K * groups * channels, channels
    )
    pieces = couple_two.reshape(K, groups, quarter, groups, quarter, groups)
    mix_two = pieces.transpose(1, 0, 5, 4, 3, 2).reshape(groups, K * channels, channels)
    mix_nat = pieces.transpose(1, 2, 3, 0, 5, 4).reshape(groups, channels, K * channels)

    vmem = pl.BlockSpec(memory_space=pltpu.VMEM)
    scratch = [
        pltpu.VMEM((2 * K, grid, grid), BF16),
        pltpu.VMEM((2 * K, grid, grid), BF16),
        pltpu.VMEM((groups, grid, local * LANES), F32),
        pltpu.VMEM((groups, n, local * q_size, local * LANES), F32),
        pltpu.VMEM((groups, n, local * q_size, local * LANES), F32),
        pltpu.VMEM((groups, n, local * q_size, local * LANES), F32),
        pltpu.VMEM((grid, local * LANES), BF16),
        pltpu.VMEM((grid, local * LANES), BF16),
        pltpu.VMEM((local, grid, K * groups * LANES), BF16),
        pltpu.VMEM((local, grid, K * groups * LANES), BF16),
        pltpu.VMEM((local, K, grid, LANES), F32),
        pltpu.VMEM(mix_one.shape, BF16),
        pltpu.VMEM(mix_one.shape, BF16),
        pltpu.VMEM(mix_two.shape, BF16),
        pltpu.VMEM(mix_two.shape, BF16),
        pltpu.VMEM(mix_nat.shape, BF16),
        pltpu.VMEM(mix_nat.shape, BF16),
        pltpu.SemaphoreType.DMA,
        pltpu.SemaphoreType.DMA((groups, n)),
        pltpu.SemaphoreType.DMA((2, groups, n)),
    ]
    macs = ITERS * 2 * rows * channels * grid * K * (grid + channels)
    return pl.pallas_call(
        functools.partial(sweep_kernel, n, quarter, q_size),
        out_shape=(
            jax.ShapeDtypeStruct(source.shape, F32),
            jax.ShapeDtypeStruct((green.shape[0], channels, grid), F32),
        ),
        in_specs=[vmem] * 6 + [pl.BlockSpec(memory_space=pl.ANY)],
        out_specs=(vmem, vmem),
        scratch_shapes=scratch,
        compiler_params=pltpu.CompilerParams(
            collective_id=0, has_side_effects=True, vmem_limit_bytes=63 * 1024 * 1024
        ),
        cost_estimate=pl.CostEstimate(
            flops=6 * macs, bytes_accessed=4 * 4 * source.size, transcendentals=0
        ),
    )(table, green_t, green, mix_one, mix_two, mix_nat, source)


def spline_matrix(
    first_index, second_index, first_weight, second_weight, first_count, second_count
):
    first_grid = jnp.arange(first_count, dtype=jnp.int32)[None, :] - first_index[:, None]
    second_grid = jnp.arange(second_count, dtype=jnp.int32)[None, :] - second_index[:, None]
    first_rows = jnp.zeros(first_grid.shape, jnp.float32)
    second_rows = jnp.zeros(second_grid.shape, jnp.float32)
    for offset in range(4):
        first_rows = first_rows + jnp.where(
            first_grid == offset, first_weight[offset][:, None], jnp.float32(0.0)
        )
        second_rows = second_rows + jnp.where(
            second_grid == offset, second_weight[offset][:, None], jnp.float32(0.0)
        )
    return (first_rows[:, :, None] * second_rows[:, None, :]).reshape(
        first_index.shape[0], first_count * second_count
    )


def class_mats(couple, row_count, start):
    classes = (start + jnp.arange(row_count, dtype=jnp.int32)) % 4
    select = jax.nn.one_hot(classes, 4, dtype=jnp.float32)
    return jnp.einsum("rc,cmn->rmn", select, couple, precision=lax.Precision.HIGHEST)


def mix(mats, values):
    return jnp.einsum("rmn,rnx->rmx", mats, values, precision=lax.Precision.HIGHEST)


def interp(values, smat):
    return jnp.einsum("rcx,yx->rcy", values, smat, precision=lax.Precision.HIGHEST)


def to_send_one(values, quarter, p_size):
    rows = values.shape[0]
    q_size = values.shape[2] // p_size
    return (
        values.reshape(rows, 4, quarter, p_size, q_size)
        .transpose(3, 1, 0, 2, 4)
        .reshape(4 * p_size, rows, quarter * q_size)
    )


def from_send_one(arrived, quarter, r_size):
    rows = arrived.shape[0]
    q_size = arrived.shape[2] // quarter
    return (
        arrived.reshape(rows, r_size, 4, quarter, q_size)
        .transpose(0, 3, 2, 4, 1)
        .reshape(rows, 4 * quarter, q_size * r_size)
    )


def to_send_two(values, quarter, r_size):
    rows = values.shape[0]
    q_size = values.shape[2] // r_size
    return (
        values.reshape(rows, quarter, 4, q_size, r_size)
        .transpose(4, 2, 0, 1, 3)
        .reshape(4 * r_size, rows, quarter * q_size)
    )


def from_send_two(arrived, quarter, p_size):
    rows = arrived.shape[0]
    q_size = arrived.shape[2] // quarter
    return (
        arrived.reshape(rows, p_size, 4, quarter, q_size)
        .transpose(0, 2, 3, 1, 4)
        .reshape(rows, 4 * quarter, p_size * q_size)
    )


def shards(
    devices,
    source,
    green,
    couple_one,
    couple_two,
    p_bracket,
    q_bracket,
    p_weight,
    q_weight,
    qr_bracket,
    r_bracket,
    qr_weight,
    r_weight,
):
    rows_one = source.shape[0]
    rows_two = green.shape[0]
    quarter = source.shape[1] // 4
    here = lax.axis_index("mom")
    p_size = rows_two * devices // 4
    r_size = rows_one * devices // 4
    q_size = source.shape[2] // p_size
    first_maps = [
        spline_matrix(p_bracket[k], q_bracket[k], p_weight[k], q_weight[k], p_size, q_size)
        for k in range(K)
    ]
    second_maps = [
        spline_matrix(qr_bracket[k], r_bracket[k], qr_weight[k], r_weight[k], q_size, r_size)
        for k in range(K)
    ]
    mats_one = [class_mats(couple_one[k], rows_one, here * rows_one) for k in range(K)]
    mats_two = [class_mats(couple_two[k], rows_two, here * rows_two) for k in range(K)]
    scale = green[:, None, :]
    state = source
    component = None
    for step in range(ITERS):
        one = interp(mix(mats_one[0], state), first_maps[0])
        k = 1
        one = one + interp(mix(mats_one[k], state), first_maps[k])
        arrived = lax.all_to_all(
            to_send_one(one, quarter, p_size), "mom", split_axis=0, concat_axis=1, tiled=True
        )
        regrouped = from_send_one(arrived, quarter, r_size)
        total = mix(mats_two[0], interp(regrouped, second_maps[0]))
        k = 1
        total = total + mix(mats_two[k], interp(regrouped, second_maps[k]))
        component = scale * total
        returned = lax.all_to_all(
            to_send_two(component, quarter, r_size), "mom", split_axis=0, concat_axis=1, tiled=True
        )
        state = source + from_send_two(returned, quarter, p_size)
    return (state, component)


def solution(mesh):
    placed = (P(("energy", "mom"), None, None), P(("energy", "mom"), None)) + (P(),) * 10
    devices = mesh.shape["mom"]

    def local_part(source, green, *rest):
        rows, channels, grid = source.shape
        block_rows = rows * LANES // 4
        fits = (
            rows == green.shape[0]
            and rows == 8
            and channels == LANES
            and grid % (2 * LANES) == 0
            and devices % (grid // (2 * LANES)) == 0
            and LANES % (grid * 4 // (rows * devices)) == 0
            and block_rows == 2 * LANES
        )
        if fits:
            return fused(devices, source, green, *rest)
        return shards(devices, source, green, *rest)

    return jax.shard_map(
        local_part,
        mesh=mesh,
        in_specs=placed,
        out_specs=(P(("energy", "mom"), None, None), P(("energy", "mom"), None, None)),
        check_vma=False,
    )
```

```python
import functools

import jax
import jax.numpy as jnp
from jax import lax
from jax.experimental import pallas as pl
from jax.experimental.pallas import tpu as pltpu
from jax.sharding import PartitionSpec as P

K = 2
ITERS = 2
LANES = 128
F32 = jnp.float32
BF16 = jnp.bfloat16


def split(values):
    high = values.astype(BF16)
    return high, (values - high.astype(F32)).astype(BF16)


def dot3(a_high, a_low, b_high, b_low, dims=(((1,), (0,)), ((), ()))):
    mul = functools.partial(lax.dot_general, dimension_numbers=dims, preferred_element_type=F32)
    return mul(a_high, b_high) + (mul(a_high, b_low) + mul(a_low, b_high))


def sweep_kernel(
    n,
    quarter,
    q_size,
    source_ref,
    green_ref,
    couple_one_ref,
    couple_two_ref,
    p_bracket_ref,
    q_bracket_ref,
    p_weight_ref,
    q_weight_ref,
    qr_bracket_ref,
    r_bracket_ref,
    qr_weight_ref,
    r_weight_ref,
    amp_ref,
    comp_ref,
    map_high,
    map_low,
    start_t,
    send_buf,
    recv_one,
    recv_two,
    v_high,
    v_low,
    w_high,
    w_low,
    w_keep,
    e_high,
    e_low,
    d_high,
    d_low,
    a_high,
    a_low,
    tab_rows,
    tab,
    tab_turned,
    square,
    load_sem,
    send_sem,
    recv_sem,
):
    me = lax.axis_index("mom")
    grid = start_t.shape[1]
    groups = start_t.shape[0]
    local = start_t.shape[2] // LANES
    block = 2 * LANES
    blocks = grid // block
    block_dests = n // blocks
    per_tile = LANES // q_size
    half = groups * LANES
    outer_size = grid // q_size

    load = pltpu.make_async_copy(source_ref, amp_ref, load_sem)
    load.start()

    def xor(left, right):
        out, unit = 0, 1
        while unit < n:
            x, y = (left // unit) % 2, (right // unit) % 2
            out = out + unit * (x + y - 2 * x * y)
            unit *= 2
        return out

    barrier = pltpu.get_barrier_semaphore()

    def greet(offset, carry):
        pl.semaphore_signal(
            barrier,
            inc=1,
            device_id={"mom": xor(me, offset)},
            device_id_type=pl.DeviceIdType.MESH,
        )
        return carry

    lax.fori_loop(1, n, greet, 0)

    def rows_of(i, size=block):
        return pl.ds(pl.multiple_of(i * size, size), size)

    tab_rows[...] = jnp.zeros_like(tab_rows)
    for k in range(K):
        for slot, refs in (
            (k, (p_bracket_ref, q_bracket_ref, p_weight_ref, q_weight_ref)),
            (K + k, (r_bracket_ref, qr_bracket_ref, r_weight_ref, qr_weight_ref)),
        ):
            at = 10 * slot
            tab_rows[at : at + 1, :] = refs[0][k : k + 1, :].astype(F32)
            tab_rows[at + 1 : at + 2, :] = refs[1][k : k + 1, :].astype(F32)
            tab_rows[at + 2 : at + 6, :] = refs[2][k]
            tab_rows[at + 6 : at + 10, :] = refs[3][k]
    green_at = 20 * K
    tab_rows[green_at : green_at + local * groups, :] = green_ref[...]
    tab[...] = tab_rows[...].T

    def build_map(slot, i, table_ref):
        base = 10 * slot
        rows = rows_of(i)
        table = table_ref[rows, :]

        def col(j):
            return jnp.broadcast_to(table[:, base + j : base + j + 1], (block, LANES))

        first, second = col(0), col(1)
        w_first = [col(2 + j) for j in range(4)]
        w_second = [col(6 + j) for j in range(4)]
        lane = lax.broadcasted_iota(jnp.int32, (block, LANES), 1)
        fine = (lane % q_size).astype(F32) - second
        coarse = (lane // q_size).astype(F32) - first
        zero = jnp.zeros((block, LANES), F32)
        inner = zero
        for j in range(4):
            inner = inner + jnp.where(fine == j, w_second[j], zero)
        for t in range(grid // LANES):
            here = coarse + F32(per_tile * t)
            outer = zero
            for j in range(4):
                outer = outer + jnp.where(here == j, w_first[j], zero)
            high, low = split(outer * inner)
            map_high[slot, rows, t * LANES : (t + 1) * LANES] = high
            map_low[slot, rows, t * LANES : (t + 1) * LANES] = low

    def copy_of(phase, g, offset):
        dest = xor(me, offset)
        into = recv_one if phase == 0 else recv_two
        return pltpu.make_async_remote_copy(
            src_ref=send_buf.at[g, dest],
            dst_ref=into.at[g, me],
            send_sem=send_sem.at[g, offset],
            recv_sem=recv_sem.at[phase, g, offset],
            device_id={"mom": dest},
            device_id_type=pl.DeviceIdType.MESH,
        )

    def keep_own(phase, g):
        into = recv_one if phase == 0 else recv_two
        into[g, me] = send_buf[g, me]

    def start_sends(phase, g):
        def body(t, carry):
            odd = t % 2
            offset = (1 - odd) * (n // 2 + t // 2) + odd * ((t + 1) // 2)
            copy_of(phase, g, offset).start()
            return carry

        lax.fori_loop(0, n - 1, body, 0)
        keep_own(phase, g)

    def start_block(phase, g, flip):
        for j in range(block_dests):
            if flip * block_dests + j > 0:
                copy_of(phase, g, flip * block_dests + j).start()

    flips = []
    for j in range(blocks // 2):
        flips += [blocks // 2 + j, (j + 1) % (blocks // 2)]

    def wait_sends(phase, g):
        def body(offset, carry):
            copy_of(phase, g, offset).wait_send()
            return carry

        lax.fori_loop(1, n, body, 0)

    def wait_recvs(phase, g):
        into = recv_one if phase == 0 else recv_two

        def body(offset, carry):
            origin = xor(me, offset)
            pltpu.make_async_remote_copy(
                src_ref=send_buf.at[g, origin],
                dst_ref=into.at[g, origin],
                send_sem=send_sem.at[g, offset],
                recv_sem=recv_sem.at[phase, g, offset],
                device_id={"mom": origin},
                device_id_type=pl.DeviceIdType.MESH,
            ).wait_recv()
            return carry

        lax.fori_loop(1, n, body, 0)

    def set_values(values):
        high, low = split(values)
        v_high[0] = high
        v_low[0] = low

    def place(g, i, part, out):
        out = out.reshape(block_dests, local, q_size, LANES)
        dests = pl.ds(i * block_dests, block_dests)
        for other in range(local):
            send_buf[
                g,
                dests,
                part * q_size : (part + 1) * q_size,
                other * LANES : (other + 1) * LANES,
            ] = out[:, other]

    def mix_first(g):
        def body(i, carry):
            rows = rows_of(i)
            e_both = [
                jnp.concatenate([ref[g, k * half : (k + 1) * half, :] for k in range(K)], axis=1)
                for ref in (e_high, e_low)
            ]
            for part in range(local):
                lanes = slice(part * LANES, (part + 1) * LANES)
                joined = jnp.concatenate([start_t[c, rows, lanes] for c in range(groups)], axis=1)
                high, low = split(joined)
                high, low = split(dot3(high, low, *e_both))
                for k in range(K):
                    v_high[k, rows, lanes] = high[:, k * LANES : (k + 1) * LANES]
                    v_low[k, rows, lanes] = low[:, k * LANES : (k + 1) * LANES]
            return carry

        lax.fori_loop(0, blocks, body, 0)

    def first_rows(g, i):
        rows = rows_of(i)
        out = sum(
            dot3(map_high[k, rows, :], map_low[k, rows, :], v_high[k], v_low[k]) for k in range(K)
        )
        for part in range(local):
            place(g, i, part, out[:, part * LANES : (part + 1) * LANES])

    def interp_one(g, i):
        rows = rows_of(i)
        for k in range(K):
            out = dot3(map_high[k, rows, :], map_low[k, rows, :], v_high[0], v_low[0])
            high, low = split(out)
            lanes = pl.ds(pl.multiple_of((k * groups + g) * LANES, LANES), LANES)
            for part in range(local):
                w_high[part, rows, lanes] = high[:, part * LANES : (part + 1) * LANES]
                w_low[part, rows, lanes] = low[:, part * LANES : (part + 1) * LANES]

    def mix_one(g, i):
        rows = rows_of(i)
        for part in range(local):
            out = dot3(w_high[part, rows, :], w_low[part, rows, :], e_high[g], e_low[g])
            place(g, i, part, out)

    def each_block(work):
        def body(i, carry):
            work(i)
            return carry

        lax.fori_loop(0, blocks, body, 0)

    def each_group(first, last, work):
        def body(g, carry):
            work(g)
            return carry

        lax.fori_loop(first, last, body, 0)

    def one(it):
        if it == 0:
            mix_first(0)
            pl.semaphore_wait(barrier, n - 1)
        else:

            def arrive(g):
                wait_recvs(1, g)
                set_values(start_t[g] + recv_two[g].reshape(grid, local * LANES))

            def take(g):
                arrive(g)
                each_block(functools.partial(interp_one, g))

            each_group(0, groups - 1, take)
            arrive(groups - 1)
            wait_sends(1, 0)
        for flip in flips:
            i = xor(me // block_dests, flip)
            if it == 0:
                for k in range(K):
                    build_map(k, i, tab)
                first_rows(0, i)
            else:
                interp_one(groups - 1, i)
                mix_one(0, i)
            start_block(0, 0, flip)
        keep_own(0, 0)

        def give(g):
            if it == 0:
                mix_first(g)
                each_block(functools.partial(first_rows, g))
            else:
                wait_sends(1, g)
                each_block(functools.partial(mix_one, g))
            start_sends(0, g)

        each_group(1, groups, give)

    def two(it):
        last = it == ITERS - 1

        def work(g):
            wait_recvs(0, g)
            wait_sends(0, g)
            set_values(recv_one[g].reshape(grid, local * LANES))

            def rows_body(i):
                rows = rows_of(i)
                outs = [
                    dot3(map_high[K + k, rows, :], map_low[K + k, rows, :], v_high[0], v_low[0])
                    for k in range(K)
                ]
                table = tab_turned[rows, :]
                lane = lax.broadcasted_iota(jnp.int32, table.shape, 1)
                for part in range(local):
                    lanes = slice(part * LANES, (part + 1) * LANES)
                    high, low = split(jnp.concatenate([out[:, lanes] for out in outs], axis=1))
                    mixed = dot3(high, low, d_high[g], d_low[g])
                    here = lane == green_at + part * groups + g
                    scale = jnp.sum(jnp.where(here, table, F32(0.0)), axis=1, keepdims=True)
                    place(g, i, part, mixed * scale)
                    if last:
                        for k in range(K):
                            w_keep[part, k, rows, :] = outs[k][:, lanes]

            each_block(rows_body)
            start_sends(1, g)
            if last:
                step = block // outer_size
                for part in range(local):
                    scale = green_ref[pl.ds(part * groups + g, 1), :]
                    for s in range(blocks):
                        joined = jnp.concatenate(
                            [
                                jnp.concatenate(
                                    [
                                        w_keep[part, k, pl.ds(q, outer_size, stride=q_size), :]
                                        for q in range(s * step, (s + 1) * step)
                                    ],
                                    axis=0,
                                )
                                for k in range(K)
                            ],
                            axis=1,
                        )
                        high, low = split(joined)
                        out = dot3(a_high[g], a_low[g], high, low, (((1,), (1,)), ((), ())))
                        lanes = slice(s * block, (s + 1) * block)
                        comp_ref[part * groups + g, :, lanes] = out * scale[:, lanes]

        each_group(0, groups, work)

    lane = lax.broadcasted_iota(jnp.int32, (LANES, LANES), 1)
    for k in range(K):
        for c in range(groups):
            turned = couple_one_ref[k, c].T
            for to in range(groups):
                shift = ((c - to) * quarter) % LANES
                moved = pltpu.roll(turned, shift, 1) if shift else turned
                high, low = split(jnp.where(lane // quarter == c, moved, F32(0.0)))
                for g in range(groups):
                    at = (k * groups + g) * LANES + c * quarter
                    e_high[to, at : at + quarter, :] = high[g * quarter : (g + 1) * quarter]
                    e_low[to, at : at + quarter, :] = low[g * quarter : (g + 1) * quarter]
    load.wait()

    def transpose_in(g):
        chans = pl.ds(pl.multiple_of(g * quarter, quarter), quarter)
        for part in range(local):
            stacked = jnp.concatenate(
                [amp_ref[part * groups + c, chans, :] for c in range(groups)], axis=0
            )
            start_t[g, :, part * LANES : (part + 1) * LANES] = stacked.T

    each_group(0, groups, transpose_in)
    one(0)

    for r in range(outer_size):
        tab_turned[r * q_size : (r + 1) * q_size, :] = tab[pl.ds(r, q_size, stride=outer_size), :]

    def build_two(i):
        for k in range(K):
            build_map(K + k, i, tab_turned)

    each_block(build_two)

    def picked(load):
        return jnp.concatenate(
            [load(pl.ds(c, quarter, stride=groups)) for c in range(groups)], axis=0
        )

    def couple(g):
        for k in range(K):
            square[...] = picked(lambda rows: couple_two_ref[k, g, rows, :]).T
            high, low = split(picked(lambda rows: square[rows, :]))
            d_high[g, k * LANES : (k + 1) * LANES, :] = high
            d_low[g, k * LANES : (k + 1) * LANES, :] = low
            square[...] = couple_two_ref[k, g].T
            high, low = split(picked(lambda rows: square[rows, :]).T)
            a_high[g, :, k * LANES : (k + 1) * LANES] = high
            a_low[g, :, k * LANES : (k + 1) * LANES] = low

    each_group(0, groups, couple)
    two(0)
    for it in range(1, ITERS):
        one(it)
        two(it)

    def finish(g):
        wait_recvs(1, g)
        total = start_t[g] + recv_two[g].reshape(grid, local * LANES)
        chans = pl.ds(pl.multiple_of(g * quarter, quarter), quarter)
        for part in range(local):
            turned = total[:, part * LANES : (part + 1) * LANES].T
            for c in range(groups):
                amp_ref[part * groups + c, chans, :] = turned[c * quarter : (c + 1) * quarter]
        wait_sends(1, g)

    each_group(0, groups, finish)


def fused(n, source, green, couple_one, couple_two, *tables):
    rows, channels, grid = source.shape
    groups = couple_one.shape[1]
    quarter = channels // groups
    local = rows // groups
    q_size = grid // (rows * n // groups)

    vmem = pl.BlockSpec(memory_space=pltpu.VMEM)
    boxes = (groups, n, local * q_size, local * LANES)
    scratch = [
        pltpu.VMEM((2 * K, grid, grid), BF16),
        pltpu.VMEM((2 * K, grid, grid), BF16),
        pltpu.VMEM((groups, grid, local * LANES), F32),
        pltpu.VMEM(boxes, F32),
        pltpu.VMEM(boxes, F32),
        pltpu.VMEM(boxes, F32),
        pltpu.VMEM((K, grid, local * LANES), BF16),
        pltpu.VMEM((K, grid, local * LANES), BF16),
        pltpu.VMEM((local, grid, K * groups * LANES), BF16),
        pltpu.VMEM((local, grid, K * groups * LANES), BF16),
        pltpu.VMEM((local, K, grid, LANES), F32),
        pltpu.VMEM((groups, K * groups * LANES, LANES), BF16),
        pltpu.VMEM((groups, K * groups * LANES, LANES), BF16),
        pltpu.VMEM((groups, K * LANES, LANES), BF16),
        pltpu.VMEM((groups, K * LANES, LANES), BF16),
        pltpu.VMEM((groups, LANES, K * LANES), BF16),
        pltpu.VMEM((groups, LANES, K * LANES), BF16),
        pltpu.VMEM((LANES, grid), F32),
        pltpu.VMEM((grid, LANES), F32),
        pltpu.VMEM((grid, LANES), F32),
        pltpu.VMEM((LANES, LANES), F32),
        pltpu.SemaphoreType.DMA,
        pltpu.SemaphoreType.DMA((groups, n)),
        pltpu.SemaphoreType.DMA((2, groups, n)),
    ]
    macs = ITERS * 2 * rows * channels * grid * K * (grid + channels)
    return pl.pallas_call(
        functools.partial(sweep_kernel, n, quarter, q_size),
        out_shape=(
            jax.ShapeDtypeStruct(source.shape, F32),
            jax.ShapeDtypeStruct((green.shape[0], channels, grid), F32),
        ),
        in_specs=[pl.BlockSpec(memory_space=pl.ANY)] + [vmem] * (3 + len(tables)),
        out_specs=(vmem, vmem),
        scratch_shapes=scratch,
        compiler_params=pltpu.CompilerParams(
            collective_id=0, has_side_effects=True, vmem_limit_bytes=63 * 1024 * 1024
        ),
        cost_estimate=pl.CostEstimate(
            flops=6 * macs, bytes_accessed=4 * 4 * source.size, transcendentals=0
        ),
    )(source, green, couple_one, couple_two, *tables)


def spline_matrix(
    first_index, second_index, first_weight, second_weight, first_count, second_count
):
    first_grid = jnp.arange(first_count, dtype=jnp.int32)[None, :] - first_index[:, None]
    second_grid = jnp.arange(second_count, dtype=jnp.int32)[None, :] - second_index[:, None]
    first_rows = jnp.zeros(first_grid.shape, jnp.float32)
    second_rows = jnp.zeros(second_grid.shape, jnp.float32)
    for offset in range(4):
        first_rows = first_rows + jnp.where(
            first_grid == offset, first_weight[offset][:, None], jnp.float32(0.0)
        )
        second_rows = second_rows + jnp.where(
            second_grid == offset, second_weight[offset][:, None], jnp.float32(0.0)
        )
    return (first_rows[:, :, None] * second_rows[:, None, :]).reshape(
        first_index.shape[0], first_count * second_count
    )


def class_mats(couple, row_count, start):
    classes = (start + jnp.arange(row_count, dtype=jnp.int32)) % 4
    select = jax.nn.one_hot(classes, 4, dtype=jnp.float32)
    return jnp.einsum("rc,cmn->rmn", select, couple, precision=lax.Precision.HIGHEST)


def mix(mats, values):
    return jnp.einsum("rmn,rnx->rmx", mats, values, precision=lax.Precision.HIGHEST)


def interp(values, smat):
    return jnp.einsum("rcx,yx->rcy", values, smat, precision=lax.Precision.HIGHEST)


def to_send_one(values, quarter, p_size):
    rows = values.shape[0]
    q_size = values.shape[2] // p_size
    return (
        values.reshape(rows, 4, quarter, p_size, q_size)
        .transpose(3, 1, 0, 2, 4)
        .reshape(4 * p_size, rows, quarter * q_size)
    )


def from_send_one(arrived, quarter, r_size):
    rows = arrived.shape[0]
    q_size = arrived.shape[2] // quarter
    return (
        arrived.reshape(rows, r_size, 4, quarter, q_size)
        .transpose(0, 3, 2, 4, 1)
        .reshape(rows, 4 * quarter, q_size * r_size)
    )


def to_send_two(values, quarter, r_size):
    rows = values.shape[0]
    q_size = values.shape[2] // r_size
    return (
        values.reshape(rows, quarter, 4, q_size, r_size)
        .transpose(4, 2, 0, 1, 3)
        .reshape(4 * r_size, rows, quarter * q_size)
    )


def from_send_two(arrived, quarter, p_size):
    rows = arrived.shape[0]
    q_size = arrived.shape[2] // quarter
    return (
        arrived.reshape(rows, p_size, 4, quarter, q_size)
        .transpose(0, 2, 3, 1, 4)
        .reshape(rows, 4 * quarter, p_size * q_size)
    )


def shards(
    devices,
    source,
    green,
    couple_one,
    couple_two,
    p_bracket,
    q_bracket,
    p_weight,
    q_weight,
    qr_bracket,
    r_bracket,
    qr_weight,
    r_weight,
):
    rows_one = source.shape[0]
    rows_two = green.shape[0]
    quarter = source.shape[1] // 4
    here = lax.axis_index("mom")
    p_size = rows_two * devices // 4
    r_size = rows_one * devices // 4
    q_size = source.shape[2] // p_size
    first_maps = [
        spline_matrix(p_bracket[k], q_bracket[k], p_weight[k], q_weight[k], p_size, q_size)
        for k in range(K)
    ]
    second_maps = [
        spline_matrix(qr_bracket[k], r_bracket[k], qr_weight[k], r_weight[k], q_size, r_size)
        for k in range(K)
    ]
    mats_one = [class_mats(couple_one[k], rows_one, here * rows_one) for k in range(K)]
    mats_two = [class_mats(couple_two[k], rows_two, here * rows_two) for k in range(K)]
    scale = green[:, None, :]
    state = source
    component = None
    for step in range(ITERS):
        one = interp(mix(mats_one[0], state), first_maps[0])
        k = 1
        one = one + interp(mix(mats_one[k], state), first_maps[k])
        arrived = lax.all_to_all(
            to_send_one(one, quarter, p_size), "mom", split_axis=0, concat_axis=1, tiled=True
        )
        regrouped = from_send_one(arrived, quarter, r_size)
        total = mix(mats_two[0], interp(regrouped, second_maps[0]))
        k = 1
        total = total + mix(mats_two[k], interp(regrouped, second_maps[k]))
        component = scale * total
        returned = lax.all_to_all(
            to_send_two(component, quarter, r_size), "mom", split_axis=0, concat_axis=1, tiled=True
        )
        state = source + from_send_two(returned, quarter, p_size)
    return (state, component)


def solution(mesh):
    placed = (P(("energy", "mom"), None, None), P(("energy", "mom"), None)) + (P(),) * 10
    devices = mesh.shape["mom"]

    def local_part(source, green, *rest):
        rows, channels, grid = source.shape
        block_rows = rows * LANES // 4
        fits = (
            rows == green.shape[0]
            and rows == 8
            and channels == LANES
            and grid % (2 * LANES) == 0
            and grid // (2 * LANES) in (2, 4, 8, 16)
            and devices in (8, 16, 32, 64)
            and devices % (grid // (2 * LANES)) == 0
            and LANES % (grid * 4 // (rows * devices)) == 0
            and block_rows == 2 * LANES
        )
        if fits:
            return fused(devices, source, green, *rest)
        return shards(devices, source, green, *rest)

    return jax.shard_map(
        local_part,
        mesh=mesh,
        in_specs=placed,
        out_specs=(P(("energy", "mom"), None, None), P(("energy", "mom"), None, None)),
        check_vma=False,
    )
```

```python
import functools

import jax
import jax.numpy as jnp
from jax import lax
from jax.experimental import pallas as pl
from jax.experimental.pallas import tpu as pltpu
from jax.sharding import PartitionSpec as P

K = 2
ITERS = 2
LANES = 128
F32 = jnp.float32
BF16 = jnp.bfloat16


def split(values):
    high = values.astype(BF16)
    return high, (values - high.astype(F32)).astype(BF16)


def dot3(a_high, a_low, b_high, b_low, dims=(((1,), (0,)), ((), ()))):
    mul = functools.partial(lax.dot_general, dimension_numbers=dims, preferred_element_type=F32)
    return mul(a_high, b_high) + (mul(a_high, b_low) + mul(a_low, b_high))


def sweep_kernel(
    n,
    quarter,
    q_size,
    source_ref,
    green_ref,
    couple_one_ref,
    couple_two_ref,
    p_bracket_ref,
    q_bracket_ref,
    p_weight_ref,
    q_weight_ref,
    qr_bracket_ref,
    r_bracket_ref,
    qr_weight_ref,
    r_weight_ref,
    amp_out,
    comp_out,
    amp_ref,
    comp_ref,
    map_high,
    map_low,
    start_t,
    send_buf,
    recv_one,
    recv_two,
    v_high,
    v_low,
    w_high,
    w_low,
    w_keep,
    e_high,
    e_low,
    d_high,
    d_low,
    a_high,
    a_low,
    tab_rows,
    tab,
    tab_turned,
    square,
    load_sem,
    amp_sem,
    comp_sem,
    send_sem,
    recv_sem,
):
    me = lax.axis_index("mom")
    grid = start_t.shape[1]
    groups = start_t.shape[0]
    local = start_t.shape[2] // LANES
    block = 2 * LANES
    blocks = grid // block
    block_dests = n // blocks
    per_tile = LANES // q_size
    half = groups * LANES
    outer_size = grid // q_size

    def load_of(part):
        rows = pl.ds(part * groups, groups)
        return pltpu.make_async_copy(source_ref.at[rows], amp_ref.at[rows], load_sem.at[part])

    for part in range(local):
        load_of(part).start()

    def xor(left, right):
        out, unit = 0, 1
        while unit < n:
            x, y = (left // unit) % 2, (right // unit) % 2
            out = out + unit * (x + y - 2 * x * y)
            unit *= 2
        return out

    barrier = pltpu.get_barrier_semaphore()

    def greet(offset, carry):
        pl.semaphore_signal(
            barrier,
            inc=1,
            device_id={"mom": xor(me, offset)},
            device_id_type=pl.DeviceIdType.MESH,
        )
        return carry

    lax.fori_loop(1, n, greet, 0)

    def rows_of(i, size=block):
        return pl.ds(pl.multiple_of(i * size, size), size)

    tab_rows[...] = jnp.zeros_like(tab_rows)
    for k in range(K):
        for slot, refs in (
            (k, (p_bracket_ref, q_bracket_ref, p_weight_ref, q_weight_ref)),
            (K + k, (r_bracket_ref, qr_bracket_ref, r_weight_ref, qr_weight_ref)),
        ):
            at = 10 * slot
            tab_rows[at : at + 1, :] = refs[0][k : k + 1, :].astype(F32)
            tab_rows[at + 1 : at + 2, :] = refs[1][k : k + 1, :].astype(F32)
            tab_rows[at + 2 : at + 6, :] = refs[2][k]
            tab_rows[at + 6 : at + 10, :] = refs[3][k]
    green_at = 20 * K
    tab_rows[green_at : green_at + local * groups, :] = green_ref[...]
    tab[...] = tab_rows[...].T

    def build_map(slot, i, table_ref):
        base = 10 * slot
        rows = rows_of(i)
        table = table_ref[rows, :]

        def col(j):
            return jnp.broadcast_to(table[:, base + j : base + j + 1], (block, LANES))

        first, second = col(0), col(1)
        w_first = [col(2 + j) for j in range(4)]
        w_second = [col(6 + j) for j in range(4)]
        lane = lax.broadcasted_iota(jnp.int32, (block, LANES), 1)
        fine = (lane % q_size).astype(F32) - second
        coarse = (lane // q_size).astype(F32) - first
        zero = jnp.zeros((block, LANES), F32)
        inner = zero
        for j in range(4):
            inner = inner + jnp.where(fine == j, w_second[j], zero)
        for t in range(grid // LANES):
            here = coarse + F32(per_tile * t)
            outer = zero
            for j in range(4):
                outer = outer + jnp.where(here == j, w_first[j], zero)
            high, low = split(outer * inner)
            map_high[slot, rows, t * LANES : (t + 1) * LANES] = high
            map_low[slot, rows, t * LANES : (t + 1) * LANES] = low

    def half_of(ref, phase, g, box, part):
        if phase == 0:
            return ref.at[g, box, pl.ds(part * q_size, q_size)]
        return ref.at[g, box, :, pl.ds(part * LANES, LANES)]

    def copy_of(phase, g, part, offset, box=None):
        peer = xor(me, offset)
        into = recv_one if phase == 0 else recv_two
        return pltpu.make_async_remote_copy(
            src_ref=half_of(send_buf, phase, g, peer, part),
            dst_ref=half_of(into, phase, g, me if box is None else box, part),
            send_sem=send_sem.at[g, part, offset],
            recv_sem=recv_sem.at[phase, g, part, offset],
            device_id={"mom": peer},
            device_id_type=pl.DeviceIdType.MESH,
        )

    def keep_own(phase, g):
        into = recv_one if phase == 0 else recv_two
        into[g, me] = send_buf[g, me]

    def start_sends(phase, g):
        for part in range(local):

            def body(t, carry):
                odd = t % 2
                offset = (1 - odd) * (n // 2 + t // 2) + odd * ((t + 1) // 2)
                copy_of(phase, g, part, offset).start()
                return carry

            lax.fori_loop(0, n - 1, body, 0)
        keep_own(phase, g)

    def start_block(phase, g, part, flip):
        for j in range(block_dests):
            if flip * block_dests + j > 0:
                copy_of(phase, g, part, flip * block_dests + j).start()

    flips = []
    for j in range(blocks // 2):
        flips += [blocks // 2 + j, (j + 1) % (blocks // 2)]

    def wait_sends(phase, g):
        def body(offset, carry):
            for part in range(local):
                copy_of(phase, g, part, offset).wait_send()
            return carry

        lax.fori_loop(1, n, body, 0)

    def wait_half(phase, g, part):
        def body(offset, carry):
            copy_of(phase, g, part, offset, xor(me, offset)).wait_recv()
            return carry

        lax.fori_loop(1, n, body, 0)

    def wait_recvs(phase, g):
        for part in range(local):
            wait_half(phase, g, part)

    def set_values(values):
        high, low = split(values)
        v_high[0] = high
        v_low[0] = low

    def place(g, i, part, out):
        out = out.reshape(block_dests, local, q_size, LANES)
        dests = pl.ds(i * block_dests, block_dests)
        for other in range(local):
            send_buf[
                g,
                dests,
                part * q_size : (part + 1) * q_size,
                other * LANES : (other + 1) * LANES,
            ] = out[:, other]

    def mix_first(g, parts=range(local)):
        def body(i, carry):
            rows = rows_of(i)
            e_both = [
                jnp.concatenate([ref[g, k * half : (k + 1) * half, :] for k in range(K)], axis=1)
                for ref in (e_high, e_low)
            ]
            for part in parts:
                lanes = slice(part * LANES, (part + 1) * LANES)
                joined = jnp.concatenate([start_t[c, rows, lanes] for c in range(groups)], axis=1)
                high, low = split(joined)
                high, low = split(dot3(high, low, *e_both))
                for k in range(K):
                    v_high[k, rows, lanes] = high[:, k * LANES : (k + 1) * LANES]
                    v_low[k, rows, lanes] = low[:, k * LANES : (k + 1) * LANES]
            return carry

        lax.fori_loop(0, blocks, body, 0)

    def lanes_of(parts):
        return slice(parts[0] * LANES, (parts[-1] + 1) * LANES)

    def first_rows(g, i, parts=range(local)):
        rows, lanes = rows_of(i), lanes_of(parts)
        out = sum(
            dot3(map_high[k, rows, :], map_low[k, rows, :], v_high[k, :, lanes], v_low[k, :, lanes])
            for k in range(K)
        )
        for at, part in enumerate(parts):
            place(g, i, part, out[:, at * LANES : (at + 1) * LANES])

    def interp_one(g, i, parts=range(local)):
        rows, lanes = rows_of(i), lanes_of(parts)
        for k in range(K):
            out = dot3(
                map_high[k, rows, :], map_low[k, rows, :], v_high[0, :, lanes], v_low[0, :, lanes]
            )
            high, low = split(out)
            into = pl.ds(pl.multiple_of((k * groups + g) * LANES, LANES), LANES)
            for at, part in enumerate(parts):
                w_high[part, rows, into] = high[:, at * LANES : (at + 1) * LANES]
                w_low[part, rows, into] = low[:, at * LANES : (at + 1) * LANES]

    def mix_one(g, i, parts=range(local)):
        rows = rows_of(i)
        for part in parts:
            out = dot3(w_high[part, rows, :], w_low[part, rows, :], e_high[g], e_low[g])
            place(g, i, part, out)

    def each_block(work):
        def body(i, carry):
            work(i)
            return carry

        lax.fori_loop(0, blocks, body, 0)

    def each_group(first, last, work):
        def body(g, carry):
            work(g)
            return carry

        lax.fori_loop(first, last, body, 0)

    def one(it):
        last_group = groups - 1
        if it > 0:

            def take(g):
                wait_recvs(1, g)
                set_values(start_t[g] + recv_two[g].reshape(grid, local * LANES))
                each_block(functools.partial(interp_one, g))

            each_group(0, last_group, take)
            wait_sends(1, 0)
        for part in range(local):
            lanes = lanes_of([part])
            if it == 0:
                transpose_in(part)
                mix_first(0, [part])
                if part == 0:
                    pl.semaphore_wait(barrier, n - 1)
            else:
                wait_half(1, last_group, part)
                arrived = recv_two[last_group, :, :, lanes].reshape(grid, LANES)
                high, low = split(start_t[last_group, :, lanes] + arrived)
                v_high[0, :, lanes] = high
                v_low[0, :, lanes] = low
            for flip in flips:
                i = xor(me // block_dests, flip)
                if it == 0:
                    if part == 0 and flip != flips[0]:
                        for k in range(K):
                            build_map(k, i, tab)
                    first_rows(0, i, [part])
                else:
                    interp_one(last_group, i, [part])
                    mix_one(0, i, [part])
                start_block(0, 0, part, flip)
        keep_own(0, 0)

        def give(g):
            if it == 0:
                mix_first(g)
                each_block(functools.partial(first_rows, g))
            else:
                wait_sends(1, g)
                each_block(functools.partial(mix_one, g))
            start_sends(0, g)

        each_group(1, groups, give)

    def comp_copy(g, part):
        row = part * groups + g
        return pltpu.make_async_copy(comp_ref.at[row], comp_out.at[row], comp_sem.at[g, part])

    def two(it):
        last = it == ITERS - 1

        def work(g):
            wait_recvs(0, g)
            wait_sends(0, g)
            set_values(recv_one[g].reshape(grid, local * LANES))

            def rows_body(i):
                rows = rows_of(i)
                outs = [
                    dot3(map_high[K + k, rows, :], map_low[K + k, rows, :], v_high[0], v_low[0])
                    for k in range(K)
                ]
                table = tab_turned[rows, :]
                lane = lax.broadcasted_iota(jnp.int32, table.shape, 1)
                for part in range(local):
                    lanes = slice(part * LANES, (part + 1) * LANES)
                    high, low = split(jnp.concatenate([out[:, lanes] for out in outs], axis=1))
                    mixed = dot3(high, low, d_high[g], d_low[g])
                    here = lane == green_at + part * groups + g
                    scale = jnp.sum(jnp.where(here, table, F32(0.0)), axis=1, keepdims=True)
                    place(g, i, part, mixed * scale)
                    if last:
                        for k in range(K):
                            w_keep[part, k, rows, :] = outs[k][:, lanes]

            each_block(rows_body)
            start_sends(1, g)
            if last:
                step = block // outer_size
                for part in range(local):
                    scale = green_ref[pl.ds(part * groups + g, 1), :]
                    for s in range(blocks):
                        joined = jnp.concatenate(
                            [
                                jnp.concatenate(
                                    [
                                        w_keep[part, k, pl.ds(q, outer_size, stride=q_size), :]
                                        for q in range(s * step, (s + 1) * step)
                                    ],
                                    axis=0,
                                )
                                for k in range(K)
                            ],
                            axis=1,
                        )
                        high, low = split(joined)
                        out = dot3(a_high[g], a_low[g], high, low, (((1,), (1,)), ((), ())))
                        lanes = slice(s * block, (s + 1) * block)
                        comp_ref[part * groups + g, :, lanes] = out * scale[:, lanes]
                    comp_copy(g, part).start()

        each_group(0, groups, work)

    lane = lax.broadcasted_iota(jnp.int32, (LANES, LANES), 1)
    for k in range(K):
        for c in range(groups):
            turned = couple_one_ref[k, c].T
            for to in range(groups):
                shift = ((c - to) * quarter) % LANES
                moved = pltpu.roll(turned, shift, 1) if shift else turned
                high, low = split(jnp.where(lane // quarter == c, moved, F32(0.0)))
                for g in range(groups):
                    at = (k * groups + g) * LANES + c * quarter
                    e_high[to, at : at + quarter, :] = high[g * quarter : (g + 1) * quarter]
                    e_low[to, at : at + quarter, :] = low[g * quarter : (g + 1) * quarter]
    for k in range(K):
        build_map(k, xor(me // block_dests, flips[0]), tab)

    def transpose_in(part):
        load_of(part).wait()

        def body(g):
            chans = pl.ds(pl.multiple_of(g * quarter, quarter), quarter)
            stacked = jnp.concatenate(
                [amp_ref[part * groups + c, chans, :] for c in range(groups)], axis=0
            )
            start_t[g, :, part * LANES : (part + 1) * LANES] = stacked.T

        each_group(0, groups, body)

    one(0)

    for r in range(outer_size):
        tab_turned[r * q_size : (r + 1) * q_size, :] = tab[pl.ds(r, q_size, stride=outer_size), :]

    def build_two(i):
        for k in range(K):
            build_map(K + k, i, tab_turned)

    each_block(build_two)

    def picked(load):
        return jnp.concatenate(
            [load(pl.ds(c, quarter, stride=groups)) for c in range(groups)], axis=0
        )

    def couple(g):
        for k in range(K):
            square[...] = picked(lambda rows: couple_two_ref[k, g, rows, :]).T
            high, low = split(picked(lambda rows: square[rows, :]))
            d_high[g, k * LANES : (k + 1) * LANES, :] = high
            d_low[g, k * LANES : (k + 1) * LANES, :] = low
            square[...] = couple_two_ref[k, g].T
            high, low = split(picked(lambda rows: square[rows, :]).T)
            a_high[g, :, k * LANES : (k + 1) * LANES] = high
            a_low[g, :, k * LANES : (k + 1) * LANES] = low

    each_group(0, groups, couple)
    two(0)
    for it in range(1, ITERS):
        one(it)
        two(it)

    def amp_copy(g, part):
        box = (pl.ds(part * groups, groups), pl.ds(pl.multiple_of(g * quarter, quarter), quarter))
        return pltpu.make_async_copy(amp_ref.at[box], amp_out.at[box], amp_sem.at[g, part])

    def finish(g):
        chans = pl.ds(pl.multiple_of(g * quarter, quarter), quarter)
        for part in range(local):
            wait_half(1, g, part)
            lanes = lanes_of([part])
            turned = (start_t[g, :, lanes] + recv_two[g, :, :, lanes].reshape(grid, LANES)).T
            for c in range(groups):
                amp_ref[part * groups + c, chans, :] = turned[c * quarter : (c + 1) * quarter]
            amp_copy(g, part).start()

    each_group(0, groups, finish)

    def drain(g):
        wait_sends(1, g)
        for part in range(local):
            amp_copy(g, part).wait()
            comp_copy(g, part).wait()

    each_group(0, groups, drain)


def fused(n, source, green, couple_one, couple_two, *tables):
    rows, channels, grid = source.shape
    groups = couple_one.shape[1]
    quarter = channels // groups
    local = rows // groups
    q_size = grid // (rows * n // groups)

    vmem = pl.BlockSpec(memory_space=pltpu.VMEM)
    boxes = (groups, n, local * q_size, local * LANES)
    scratch = [
        pltpu.VMEM(source.shape, F32),
        pltpu.VMEM((green.shape[0], channels, grid), F32),
        pltpu.VMEM((2 * K, grid, grid), BF16),
        pltpu.VMEM((2 * K, grid, grid), BF16),
        pltpu.VMEM((groups, grid, local * LANES), F32),
        pltpu.VMEM(boxes, F32),
        pltpu.VMEM(boxes, F32),
        pltpu.VMEM(boxes, F32),
        pltpu.VMEM((K, grid, local * LANES), BF16),
        pltpu.VMEM((K, grid, local * LANES), BF16),
        pltpu.VMEM((local, grid, K * groups * LANES), BF16),
        pltpu.VMEM((local, grid, K * groups * LANES), BF16),
        pltpu.VMEM((local, K, grid, LANES), F32),
        pltpu.VMEM((groups, K * groups * LANES, LANES), BF16),
        pltpu.VMEM((groups, K * groups * LANES, LANES), BF16),
        pltpu.VMEM((groups, K * LANES, LANES), BF16),
        pltpu.VMEM((groups, K * LANES, LANES), BF16),
        pltpu.VMEM((groups, LANES, K * LANES), BF16),
        pltpu.VMEM((groups, LANES, K * LANES), BF16),
        pltpu.VMEM((LANES, grid), F32),
        pltpu.VMEM((grid, LANES), F32),
        pltpu.VMEM((grid, LANES), F32),
        pltpu.VMEM((LANES, LANES), F32),
        pltpu.SemaphoreType.DMA((local,)),
        pltpu.SemaphoreType.DMA((groups, local)),
        pltpu.SemaphoreType.DMA((groups, local)),
        pltpu.SemaphoreType.DMA((groups, local, n)),
        pltpu.SemaphoreType.DMA((2, groups, local, n)),
    ]
    macs = ITERS * 2 * rows * channels * grid * K * (grid + channels)
    return pl.pallas_call(
        functools.partial(sweep_kernel, n, quarter, q_size),
        out_shape=(
            jax.ShapeDtypeStruct(source.shape, F32),
            jax.ShapeDtypeStruct((green.shape[0], channels, grid), F32),
        ),
        in_specs=[pl.BlockSpec(memory_space=pl.ANY)] + [vmem] * (3 + len(tables)),
        out_specs=(pl.BlockSpec(memory_space=pl.ANY),) * 2,
        scratch_shapes=scratch,
        compiler_params=pltpu.CompilerParams(
            collective_id=0, has_side_effects=True, vmem_limit_bytes=63 * 1024 * 1024
        ),
        cost_estimate=pl.CostEstimate(
            flops=6 * macs, bytes_accessed=4 * 4 * source.size, transcendentals=0
        ),
    )(source, green, couple_one, couple_two, *tables)


def spline_matrix(
    first_index, second_index, first_weight, second_weight, first_count, second_count
):
    first_grid = jnp.arange(first_count, dtype=jnp.int32)[None, :] - first_index[:, None]
    second_grid = jnp.arange(second_count, dtype=jnp.int32)[None, :] - second_index[:, None]
    first_rows = jnp.zeros(first_grid.shape, jnp.float32)
    second_rows = jnp.zeros(second_grid.shape, jnp.float32)
    for offset in range(4):
        first_rows = first_rows + jnp.where(
            first_grid == offset, first_weight[offset][:, None], jnp.float32(0.0)
        )
        second_rows = second_rows + jnp.where(
            second_grid == offset, second_weight[offset][:, None], jnp.float32(0.0)
        )
    return (first_rows[:, :, None] * second_rows[:, None, :]).reshape(
        first_index.shape[0], first_count * second_count
    )


def class_mats(couple, row_count, start):
    classes = (start + jnp.arange(row_count, dtype=jnp.int32)) % 4
    select = jax.nn.one_hot(classes, 4, dtype=jnp.float32)
    return jnp.einsum("rc,cmn->rmn", select, couple, precision=lax.Precision.HIGHEST)


def mix(mats, values):
    return jnp.einsum("rmn,rnx->rmx", mats, values, precision=lax.Precision.HIGHEST)


def interp(values, smat):
    return jnp.einsum("rcx,yx->rcy", values, smat, precision=lax.Precision.HIGHEST)


def to_send_one(values, quarter, p_size):
    rows = values.shape[0]
    q_size = values.shape[2] // p_size
    return (
        values.reshape(rows, 4, quarter, p_size, q_size)
        .transpose(3, 1, 0, 2, 4)
        .reshape(4 * p_size, rows, quarter * q_size)
    )


def from_send_one(arrived, quarter, r_size):
    rows = arrived.shape[0]
    q_size = arrived.shape[2] // quarter
    return (
        arrived.reshape(rows, r_size, 4, quarter, q_size)
        .transpose(0, 3, 2, 4, 1)
        .reshape(rows, 4 * quarter, q_size * r_size)
    )


def to_send_two(values, quarter, r_size):
    rows = values.shape[0]
    q_size = values.shape[2] // r_size
    return (
        values.reshape(rows, quarter, 4, q_size, r_size)
        .transpose(4, 2, 0, 1, 3)
        .reshape(4 * r_size, rows, quarter * q_size)
    )


def from_send_two(arrived, quarter, p_size):
    rows = arrived.shape[0]
    q_size = arrived.shape[2] // quarter
    return (
        arrived.reshape(rows, p_size, 4, quarter, q_size)
        .transpose(0, 2, 3, 1, 4)
        .reshape(rows, 4 * quarter, p_size * q_size)
    )


def shards(
    devices,
    source,
    green,
    couple_one,
    couple_two,
    p_bracket,
    q_bracket,
    p_weight,
    q_weight,
    qr_bracket,
    r_bracket,
    qr_weight,
    r_weight,
):
    rows_one = source.shape[0]
    rows_two = green.shape[0]
    quarter = source.shape[1] // 4
    here = lax.axis_index("mom")
    p_size = rows_two * devices // 4
    r_size = rows_one * devices // 4
    q_size = source.shape[2] // p_size
    first_maps = [
        spline_matrix(p_bracket[k], q_bracket[k], p_weight[k], q_weight[k], p_size, q_size)
        for k in range(K)
    ]
    second_maps = [
        spline_matrix(qr_bracket[k], r_bracket[k], qr_weight[k], r_weight[k], q_size, r_size)
        for k in range(K)
    ]
    mats_one = [class_mats(couple_one[k], rows_one, here * rows_one) for k in range(K)]
    mats_two = [class_mats(couple_two[k], rows_two, here * rows_two) for k in range(K)]
    scale = green[:, None, :]
    state = source
    component = None
    for step in range(ITERS):
        one = interp(mix(mats_one[0], state), first_maps[0])
        k = 1
        one = one + interp(mix(mats_one[k], state), first_maps[k])
        arrived = lax.all_to_all(
            to_send_one(one, quarter, p_size), "mom", split_axis=0, concat_axis=1, tiled=True
        )
        regrouped = from_send_one(arrived, quarter, r_size)
        total = mix(mats_two[0], interp(regrouped, second_maps[0]))
        k = 1
        total = total + mix(mats_two[k], interp(regrouped, second_maps[k]))
        component = scale * total
        returned = lax.all_to_all(
            to_send_two(component, quarter, r_size), "mom", split_axis=0, concat_axis=1, tiled=True
        )
        state = source + from_send_two(returned, quarter, p_size)
    return (state, component)


def solution(mesh):
    placed = (P(("energy", "mom"), None, None), P(("energy", "mom"), None)) + (P(),) * 10
    devices = mesh.shape["mom"]

    def local_part(source, green, *rest):
        rows, channels, grid = source.shape
        block_rows = rows * LANES // 4
        fits = (
            rows == green.shape[0]
            and rows == 8
            and channels == LANES
            and grid % (2 * LANES) == 0
            and grid // (2 * LANES) in (2, 4, 8, 16)
            and devices in (8, 16, 32, 64)
            and devices % (grid // (2 * LANES)) == 0
            and LANES % (grid * 4 // (rows * devices)) == 0
            and block_rows == 2 * LANES
        )
        if fits:
            return fused(devices, source, green, *rest)
        return shards(devices, source, green, *rest)

    return jax.shard_map(
        local_part,
        mesh=mesh,
        in_specs=placed,
        out_specs=(P(("energy", "mom"), None, None), P(("energy", "mom"), None, None)),
        check_vma=False,
    )
```

```python
import functools

import jax
import jax.numpy as jnp
from jax import lax
from jax.experimental import pallas as pl
from jax.experimental.pallas import tpu as pltpu
from jax.sharding import PartitionSpec as P

K = 2
ITERS = 2
LANES = 128
F32 = jnp.float32
BF16 = jnp.bfloat16


def split(values):
    high = values.astype(BF16)
    return high, (values - high.astype(F32)).astype(BF16)


def dot3(a_high, a_low, b_high, b_low, dims=(((1,), (0,)), ((), ()))):
    mul = functools.partial(lax.dot_general, dimension_numbers=dims, preferred_element_type=F32)
    return mul(a_high, b_high) + (mul(a_high, b_low) + mul(a_low, b_high))


def sweep_kernel(
    n,
    quarter,
    q_size,
    source_ref,
    green_ref,
    couple_one_ref,
    couple_two_ref,
    p_bracket_ref,
    q_bracket_ref,
    p_weight_ref,
    q_weight_ref,
    qr_bracket_ref,
    r_bracket_ref,
    qr_weight_ref,
    r_weight_ref,
    amp_out,
    comp_out,
    amp_ref,
    comp_ref,
    map_high,
    map_low,
    start_t,
    send_buf,
    recv_one,
    recv_two,
    v_high,
    v_low,
    w_high,
    w_low,
    w_keep,
    e_high,
    e_low,
    d_high,
    d_low,
    a_high,
    a_low,
    tab_rows,
    tab,
    tab_turned,
    square,
    load_sem,
    amp_sem,
    comp_sem,
    send_sem,
    recv_sem,
):
    me = lax.axis_index("mom")
    grid = start_t.shape[1]
    groups = start_t.shape[0]
    local = start_t.shape[2] // LANES
    block = 2 * LANES
    blocks = grid // block
    block_dests = n // blocks
    per_tile = LANES // q_size
    half = groups * LANES
    outer_size = grid // q_size

    def load_of(part):
        rows = pl.ds(part * groups, groups)
        return pltpu.make_async_copy(source_ref.at[rows], amp_ref.at[rows], load_sem.at[part])

    for part in range(local):
        load_of(part).start()

    def xor(left, right):
        out, unit = 0, 1
        while unit < n:
            x, y = (left // unit) % 2, (right // unit) % 2
            out = out + unit * (x + y - 2 * x * y)
            unit *= 2
        return out

    barrier = pltpu.get_barrier_semaphore()

    def greet(offset, carry):
        pl.semaphore_signal(
            barrier,
            inc=1,
            device_id={"mom": xor(me, offset)},
            device_id_type=pl.DeviceIdType.MESH,
        )
        return carry

    lax.fori_loop(1, n, greet, 0)

    def rows_of(i, size=block):
        return pl.ds(pl.multiple_of(i * size, size), size)

    tab_rows[...] = jnp.zeros_like(tab_rows)
    for k in range(K):
        for slot, refs in (
            (k, (p_bracket_ref, q_bracket_ref, p_weight_ref, q_weight_ref)),
            (K + k, (r_bracket_ref, qr_bracket_ref, r_weight_ref, qr_weight_ref)),
        ):
            at = 10 * slot
            tab_rows[at : at + 1, :] = refs[0][k : k + 1, :].astype(F32)
            tab_rows[at + 1 : at + 2, :] = refs[1][k : k + 1, :].astype(F32)
            tab_rows[at + 2 : at + 6, :] = refs[2][k]
            tab_rows[at + 6 : at + 10, :] = refs[3][k]
    green_at = 20 * K
    tab_rows[green_at : green_at + local * groups, :] = green_ref[...]
    tab[...] = tab_rows[...].T

    def build_map(slot, i, table_ref):
        base = 10 * slot
        rows = rows_of(i)
        table = table_ref[rows, :]

        def col(j):
            return jnp.broadcast_to(table[:, base + j : base + j + 1], (block, LANES))

        first, second = col(0), col(1)
        w_first = [col(2 + j) for j in range(4)]
        w_second = [col(6 + j) for j in range(4)]
        lane = lax.broadcasted_iota(jnp.int32, (block, LANES), 1)
        fine = (lane % q_size).astype(F32) - second
        coarse = (lane // q_size).astype(F32) - first
        zero = jnp.zeros((block, LANES), F32)
        inner = zero
        for j in range(4):
            inner = inner + jnp.where(fine == j, w_second[j], zero)
        for t in range(grid // LANES):
            here = coarse + F32(per_tile * t)
            outer = zero
            for j in range(4):
                outer = outer + jnp.where(here == j, w_first[j], zero)
            high, low = split(outer * inner)
            map_high[slot, rows, t * LANES : (t + 1) * LANES] = high
            map_low[slot, rows, t * LANES : (t + 1) * LANES] = low

    def half_of(ref, phase, g, box, part):
        if phase == 0:
            return ref.at[g, box, pl.ds(part * q_size, q_size)]
        return ref.at[g, box, :, pl.ds(part * LANES, LANES)]

    def copy_of(phase, g, part, offset, box=None):
        peer = xor(me, offset)
        into = recv_one if phase == 0 else recv_two
        return pltpu.make_async_remote_copy(
            src_ref=half_of(send_buf, phase, g, peer, part),
            dst_ref=half_of(into, phase, g, me if box is None else box, part),
            send_sem=send_sem.at[g, part, offset],
            recv_sem=recv_sem.at[phase, g, part, offset],
            device_id={"mom": peer},
            device_id_type=pl.DeviceIdType.MESH,
        )

    def keep_own(phase, g):
        into = recv_one if phase == 0 else recv_two
        into[g, me] = send_buf[g, me]

    def start_sends(phase, g):
        for part in range(local):

            def body(t, carry):
                t = t + (me % 2) * (1 - t // (n - 2)) * (1 - 2 * (t % 2))
                odd = t % 2
                offset = (1 - odd) * (n // 2 + t // 2) + odd * ((t + 1) // 2)
                copy_of(phase, g, part, offset).start()
                return carry

            lax.fori_loop(0, n - 1, body, 0)
        keep_own(phase, g)

    def start_block(phase, g, part, flip):
        def body(offset, carry):
            copy_of(phase, g, part, offset).start()
            return carry

        first = flip * block_dests
        own = 1 - (flip + blocks - 1) // blocks
        lax.fori_loop(first + own, first + block_dests, body, 0)

    def flip_at(t):
        odd = t % 2
        return (1 - odd) * (blocks // 2 + t // 2) + odd * ((t // 2 + 1) % (blocks // 2))

    def wait_sends(phase, g):
        def body(offset, carry):
            for part in range(local):
                copy_of(phase, g, part, offset).wait_send()
            return carry

        lax.fori_loop(1, n, body, 0)

    def wait_half(phase, g, part):
        def body(offset, carry):
            copy_of(phase, g, part, offset, xor(me, offset)).wait_recv()
            return carry

        lax.fori_loop(1, n, body, 0)

    def wait_recvs(phase, g):
        for part in range(local):
            wait_half(phase, g, part)

    def set_values(values):
        high, low = split(values)
        v_high[0] = high
        v_low[0] = low

    def place(g, i, part, out):
        out = out.reshape(block_dests, local, q_size, LANES)
        dests = pl.ds(i * block_dests, block_dests)
        for other in range(local):
            send_buf[
                g,
                dests,
                part * q_size : (part + 1) * q_size,
                other * LANES : (other + 1) * LANES,
            ] = out[:, other]

    def mix_first(g, parts=range(local)):
        def body(i, carry):
            rows = rows_of(i)
            e_both = [
                jnp.concatenate([ref[g, k * half : (k + 1) * half, :] for k in range(K)], axis=1)
                for ref in (e_high, e_low)
            ]
            for part in parts:
                lanes = slice(part * LANES, (part + 1) * LANES)
                joined = jnp.concatenate([start_t[c, rows, lanes] for c in range(groups)], axis=1)
                high, low = split(joined)
                high, low = split(dot3(high, low, *e_both))
                for k in range(K):
                    v_high[k, rows, lanes] = high[:, k * LANES : (k + 1) * LANES]
                    v_low[k, rows, lanes] = low[:, k * LANES : (k + 1) * LANES]
            return carry

        lax.fori_loop(0, blocks, body, 0)

    def lanes_of(parts):
        return slice(parts[0] * LANES, (parts[-1] + 1) * LANES)

    def first_rows(g, i, parts=range(local)):
        rows, lanes = rows_of(i), lanes_of(parts)
        out = sum(
            dot3(map_high[k, rows, :], map_low[k, rows, :], v_high[k, :, lanes], v_low[k, :, lanes])
            for k in range(K)
        )
        for at, part in enumerate(parts):
            place(g, i, part, out[:, at * LANES : (at + 1) * LANES])

    def interp_one(g, i, parts=range(local)):
        rows, lanes = rows_of(i), lanes_of(parts)
        for k in range(K):
            out = dot3(
                map_high[k, rows, :], map_low[k, rows, :], v_high[0, :, lanes], v_low[0, :, lanes]
            )
            high, low = split(out)
            into = pl.ds(pl.multiple_of((k * groups + g) * LANES, LANES), LANES)
            for at, part in enumerate(parts):
                w_high[part, rows, into] = high[:, at * LANES : (at + 1) * LANES]
                w_low[part, rows, into] = low[:, at * LANES : (at + 1) * LANES]

    def mix_one(g, i, parts=range(local)):
        rows = rows_of(i)
        for part in parts:
            out = dot3(w_high[part, rows, :], w_low[part, rows, :], e_high[g], e_low[g])
            place(g, i, part, out)

    def each_block(work):
        def body(i, carry):
            work(i)
            return carry

        lax.fori_loop(0, blocks, body, 0)

    def each_group(first, last, work):
        def body(g, carry):
            work(g)
            return carry

        lax.fori_loop(first, last, body, 0)

    def one(it):
        last_group = groups - 1
        if it > 0:

            def take(g):
                wait_recvs(1, g)
                set_values(start_t[g] + recv_two[g].reshape(grid, local * LANES))
                each_block(functools.partial(interp_one, g))

            each_group(0, last_group, take)
            wait_sends(1, 0)
        for part in range(local):
            lanes = lanes_of([part])
            if it == 0:
                transpose_in(part)
                mix_first(0, [part])
                if part == 0:
                    pl.semaphore_wait(barrier, n - 1)
            else:
                wait_half(1, last_group, part)
                arrived = recv_two[last_group, :, :, lanes].reshape(grid, LANES)
                high, low = split(start_t[last_group, :, lanes] + arrived)
                v_high[0, :, lanes] = high
                v_low[0, :, lanes] = low

            def give_plane(t):
                flip = flip_at(t)
                i = xor(me // block_dests, flip)
                if it == 0:
                    if part == 0:
                        for k in range(K):
                            build_map(k, i, tab)
                    first_rows(0, i, [part])
                else:
                    interp_one(last_group, i, [part])
                    mix_one(0, i, [part])
                start_block(0, 0, part, flip)

            each_block(give_plane)
        keep_own(0, 0)

        def give(g):
            if it == 0:
                mix_first(g)
                each_block(functools.partial(first_rows, g))
            else:
                wait_sends(1, g)
                each_block(functools.partial(mix_one, g))
            start_sends(0, g)

        each_group(1, groups, give)

    def comp_copy(g, part):
        row = part * groups + g
        return pltpu.make_async_copy(comp_ref.at[row], comp_out.at[row], comp_sem.at[g, part])

    def two(it):
        last = it == ITERS - 1

        def work(g):
            wait_recvs(0, g)
            wait_sends(0, g)
            set_values(recv_one[g].reshape(grid, local * LANES))

            def rows_body(i):
                rows = rows_of(i)
                outs = [
                    dot3(map_high[K + k, rows, :], map_low[K + k, rows, :], v_high[0], v_low[0])
                    for k in range(K)
                ]
                table = tab_turned[rows, :]
                lane = lax.broadcasted_iota(jnp.int32, table.shape, 1)
                for part in range(local):
                    lanes = slice(part * LANES, (part + 1) * LANES)
                    high, low = split(jnp.concatenate([out[:, lanes] for out in outs], axis=1))
                    mixed = dot3(high, low, d_high[g], d_low[g])
                    here = lane == green_at + part * groups + g
                    scale = jnp.sum(jnp.where(here, table, F32(0.0)), axis=1, keepdims=True)
                    place(g, i, part, mixed * scale)
                    if last:
                        for k in range(K):
                            w_keep[part, k, rows, :] = outs[k][:, lanes]

            each_block(rows_body)
            start_sends(1, g)
            if last:
                step = block // outer_size
                for part in range(local):
                    scale = green_ref[pl.ds(part * groups + g, 1), :]
                    for s in range(blocks):
                        joined = jnp.concatenate(
                            [
                                jnp.concatenate(
                                    [
                                        w_keep[part, k, pl.ds(q, outer_size, stride=q_size), :]
                                        for q in range(s * step, (s + 1) * step)
                                    ],
                                    axis=0,
                                )
                                for k in range(K)
                            ],
                            axis=1,
                        )
                        high, low = split(joined)
                        out = dot3(a_high[g], a_low[g], high, low, (((1,), (1,)), ((), ())))
                        lanes = slice(s * block, (s + 1) * block)
                        comp_ref[part * groups + g, :, lanes] = out * scale[:, lanes]
                    comp_copy(g, part).start()

        each_group(0, groups, work)

    lane = lax.broadcasted_iota(jnp.int32, (LANES, LANES), 1)
    for k in range(K):
        for c in range(groups):
            turned = couple_one_ref[k, c].T
            for to in range(groups):
                shift = ((c - to) * quarter) % LANES
                moved = pltpu.roll(turned, shift, 1) if shift else turned
                high, low = split(jnp.where(lane // quarter == c, moved, F32(0.0)))
                for g in range(groups):
                    at = (k * groups + g) * LANES + c * quarter
                    e_high[to, at : at + quarter, :] = high[g * quarter : (g + 1) * quarter]
                    e_low[to, at : at + quarter, :] = low[g * quarter : (g + 1) * quarter]
    def transpose_in(part):
        load_of(part).wait()

        def body(g):
            chans = pl.ds(pl.multiple_of(g * quarter, quarter), quarter)
            stacked = jnp.concatenate(
                [amp_ref[part * groups + c, chans, :] for c in range(groups)], axis=0
            )
            start_t[g, :, part * LANES : (part + 1) * LANES] = stacked.T

        each_group(0, groups, body)

    one(0)

    for r in range(outer_size):
        tab_turned[r * q_size : (r + 1) * q_size, :] = tab[pl.ds(r, q_size, stride=outer_size), :]

    def build_two(i):
        for k in range(K):
            build_map(K + k, i, tab_turned)

    each_block(build_two)

    def picked(load):
        return jnp.concatenate(
            [load(pl.ds(c, quarter, stride=groups)) for c in range(groups)], axis=0
        )

    def couple(g):
        for k in range(K):
            square[...] = picked(lambda rows: couple_two_ref[k, g, rows, :]).T
            high, low = split(picked(lambda rows: square[rows, :]))
            d_high[g, k * LANES : (k + 1) * LANES, :] = high
            d_low[g, k * LANES : (k + 1) * LANES, :] = low
            square[...] = couple_two_ref[k, g].T
            high, low = split(picked(lambda rows: square[rows, :]).T)
            a_high[g, :, k * LANES : (k + 1) * LANES] = high
            a_low[g, :, k * LANES : (k + 1) * LANES] = low

    each_group(0, groups, couple)
    two(0)
    for it in range(1, ITERS):
        one(it)
        two(it)

    def amp_copy(g, part):
        box = (pl.ds(part * groups, groups), pl.ds(pl.multiple_of(g * quarter, quarter), quarter))
        return pltpu.make_async_copy(amp_ref.at[box], amp_out.at[box], amp_sem.at[g, part])

    def finish(g):
        chans = pl.ds(pl.multiple_of(g * quarter, quarter), quarter)
        for part in range(local):
            wait_half(1, g, part)
            lanes = lanes_of([part])
            turned = (start_t[g, :, lanes] + recv_two[g, :, :, lanes].reshape(grid, LANES)).T
            for c in range(groups):
                amp_ref[part * groups + c, chans, :] = turned[c * quarter : (c + 1) * quarter]
            amp_copy(g, part).start()

    each_group(0, groups, finish)

    def drain(g):
        wait_sends(1, g)
        for part in range(local):
            amp_copy(g, part).wait()
            comp_copy(g, part).wait()

    each_group(0, groups, drain)


def fused(n, source, green, couple_one, couple_two, *tables):
    rows, channels, grid = source.shape
    groups = couple_one.shape[1]
    quarter = channels // groups
    local = rows // groups
    q_size = grid // (rows * n // groups)

    vmem = pl.BlockSpec(memory_space=pltpu.VMEM)
    boxes = (groups, n, local * q_size, local * LANES)
    scratch = [
        pltpu.VMEM(source.shape, F32),
        pltpu.VMEM((green.shape[0], channels, grid), F32),
        pltpu.VMEM((2 * K, grid, grid), BF16),
        pltpu.VMEM((2 * K, grid, grid), BF16),
        pltpu.VMEM((groups, grid, local * LANES), F32),
        pltpu.VMEM(boxes, F32),
        pltpu.VMEM(boxes, F32),
        pltpu.VMEM(boxes, F32),
        pltpu.VMEM((K, grid, local * LANES), BF16),
        pltpu.VMEM((K, grid, local * LANES), BF16),
        pltpu.VMEM((local, grid, K * groups * LANES), BF16),
        pltpu.VMEM((local, grid, K * groups * LANES), BF16),
        pltpu.VMEM((local, K, grid, LANES), F32),
        pltpu.VMEM((groups, K * groups * LANES, LANES), BF16),
        pltpu.VMEM((groups, K * groups * LANES, LANES), BF16),
        pltpu.VMEM((groups, K * LANES, LANES), BF16),
        pltpu.VMEM((groups, K * LANES, LANES), BF16),
        pltpu.VMEM((groups, LANES, K * LANES), BF16),
        pltpu.VMEM((groups, LANES, K * LANES), BF16),
        pltpu.VMEM((LANES, grid), F32),
        pltpu.VMEM((grid, LANES), F32),
        pltpu.VMEM((grid, LANES), F32),
        pltpu.VMEM((LANES, LANES), F32),
        pltpu.SemaphoreType.DMA((local,)),
        pltpu.SemaphoreType.DMA((groups, local)),
        pltpu.SemaphoreType.DMA((groups, local)),
        pltpu.SemaphoreType.DMA((groups, local, n)),
        pltpu.SemaphoreType.DMA((2, groups, local, n)),
    ]
    macs = ITERS * 2 * rows * channels * grid * K * (grid + channels)
    return pl.pallas_call(
        functools.partial(sweep_kernel, n, quarter, q_size),
        out_shape=(
            jax.ShapeDtypeStruct(source.shape, F32),
            jax.ShapeDtypeStruct((green.shape[0], channels, grid), F32),
        ),
        in_specs=[pl.BlockSpec(memory_space=pl.ANY)] + [vmem] * (3 + len(tables)),
        out_specs=(pl.BlockSpec(memory_space=pl.ANY),) * 2,
        scratch_shapes=scratch,
        compiler_params=pltpu.CompilerParams(
            collective_id=0, has_side_effects=True, vmem_limit_bytes=63 * 1024 * 1024
        ),
        cost_estimate=pl.CostEstimate(
            flops=6 * macs, bytes_accessed=4 * 4 * source.size, transcendentals=0
        ),
    )(source, green, couple_one, couple_two, *tables)


def spline_matrix(
    first_index, second_index, first_weight, second_weight, first_count, second_count
):
    first_grid = jnp.arange(first_count, dtype=jnp.int32)[None, :] - first_index[:, None]
    second_grid = jnp.arange(second_count, dtype=jnp.int32)[None, :] - second_index[:, None]
    first_rows = jnp.zeros(first_grid.shape, jnp.float32)
    second_rows = jnp.zeros(second_grid.shape, jnp.float32)
    for offset in range(4):
        first_rows = first_rows + jnp.where(
            first_grid == offset, first_weight[offset][:, None], jnp.float32(0.0)
        )
        second_rows = second_rows + jnp.where(
            second_grid == offset, second_weight[offset][:, None], jnp.float32(0.0)
        )
    return (first_rows[:, :, None] * second_rows[:, None, :]).reshape(
        first_index.shape[0], first_count * second_count
    )


def class_mats(couple, row_count, start):
    classes = (start + jnp.arange(row_count, dtype=jnp.int32)) % 4
    select = jax.nn.one_hot(classes, 4, dtype=jnp.float32)
    return jnp.einsum("rc,cmn->rmn", select, couple, precision=lax.Precision.HIGHEST)


def mix(mats, values):
    return jnp.einsum("rmn,rnx->rmx", mats, values, precision=lax.Precision.HIGHEST)


def interp(values, smat):
    return jnp.einsum("rcx,yx->rcy", values, smat, precision=lax.Precision.HIGHEST)


def to_send_one(values, quarter, p_size):
    rows = values.shape[0]
    q_size = values.shape[2] // p_size
    return (
        values.reshape(rows, 4, quarter, p_size, q_size)
        .transpose(3, 1, 0, 2, 4)
        .reshape(4 * p_size, rows, quarter * q_size)
    )


def from_send_one(arrived, quarter, r_size):
    rows = arrived.shape[0]
    q_size = arrived.shape[2] // quarter
    return (
        arrived.reshape(rows, r_size, 4, quarter, q_size)
        .transpose(0, 3, 2, 4, 1)
        .reshape(rows, 4 * quarter, q_size * r_size)
    )


def to_send_two(values, quarter, r_size):
    rows = values.shape[0]
    q_size = values.shape[2] // r_size
    return (
        values.reshape(rows, quarter, 4, q_size, r_size)
        .transpose(4, 2, 0, 1, 3)
        .reshape(4 * r_size, rows, quarter * q_size)
    )


def from_send_two(arrived, quarter, p_size):
    rows = arrived.shape[0]
    q_size = arrived.shape[2] // quarter
    return (
        arrived.reshape(rows, p_size, 4, quarter, q_size)
        .transpose(0, 2, 3, 1, 4)
        .reshape(rows, 4 * quarter, p_size * q_size)
    )


def shards(
    devices,
    source,
    green,
    couple_one,
    couple_two,
    p_bracket,
    q_bracket,
    p_weight,
    q_weight,
    qr_bracket,
    r_bracket,
    qr_weight,
    r_weight,
):
    rows_one = source.shape[0]
    rows_two = green.shape[0]
    quarter = source.shape[1] // 4
    here = lax.axis_index("mom")
    p_size = rows_two * devices // 4
    r_size = rows_one * devices // 4
    q_size = source.shape[2] // p_size
    first_maps = [
        spline_matrix(p_bracket[k], q_bracket[k], p_weight[k], q_weight[k], p_size, q_size)
        for k in range(K)
    ]
    second_maps = [
        spline_matrix(qr_bracket[k], r_bracket[k], qr_weight[k], r_weight[k], q_size, r_size)
        for k in range(K)
    ]
    mats_one = [class_mats(couple_one[k], rows_one, here * rows_one) for k in range(K)]
    mats_two = [class_mats(couple_two[k], rows_two, here * rows_two) for k in range(K)]
    scale = green[:, None, :]
    state = source
    component = None
    for step in range(ITERS):
        one = interp(mix(mats_one[0], state), first_maps[0])
        k = 1
        one = one + interp(mix(mats_one[k], state), first_maps[k])
        arrived = lax.all_to_all(
            to_send_one(one, quarter, p_size), "mom", split_axis=0, concat_axis=1, tiled=True
        )
        regrouped = from_send_one(arrived, quarter, r_size)
        total = mix(mats_two[0], interp(regrouped, second_maps[0]))
        k = 1
        total = total + mix(mats_two[k], interp(regrouped, second_maps[k]))
        component = scale * total
        returned = lax.all_to_all(
            to_send_two(component, quarter, r_size), "mom", split_axis=0, concat_axis=1, tiled=True
        )
        state = source + from_send_two(returned, quarter, p_size)
    return (state, component)


def solution(mesh):
    placed = (P(("energy", "mom"), None, None), P(("energy", "mom"), None)) + (P(),) * 10
    devices = mesh.shape["mom"]

    def local_part(source, green, *rest):
        rows, channels, grid = source.shape
        block_rows = rows * LANES // 4
        fits = (
            rows == green.shape[0]
            and rows == 8
            and channels == LANES
            and grid % (2 * LANES) == 0
            and grid // (2 * LANES) in (2, 4, 8, 16)
            and devices in (8, 16, 32, 64)
            and devices % (grid // (2 * LANES)) == 0
            and LANES % (grid * 4 // (rows * devices)) == 0
            and block_rows == 2 * LANES
        )
        if fits:
            return fused(devices, source, green, *rest)
        return shards(devices, source, green, *rest)

    return jax.shard_map(
        local_part,
        mesh=mesh,
        in_specs=placed,
        out_specs=(P(("energy", "mom"), None, None), P(("energy", "mom"), None, None)),
        check_vma=False,
    )
```
